128 devices in a mesh: group: 4 (over x), sub: 32 (over y, z, core).
Axes of the slice: x: 4, y: 4, z: 4, core: 2. Of those that a mesh axis runs over, the one named last changes fastest.
Arguments:
- a_vals: bfloat16 [4096, 9, 128, 128], P(('group', 'sub')), may hold values from -0.5 to 0.5
- a_cols: int32 [4096, 9], P(('group', 'sub')), may hold values from 0 to 47
- p_vals: bfloat16 [4096, 2, 128, 128], P(('group', 'sub')), may hold values from -0.5 to 0.5
- halo_send: int32 [2048], P(('group', 'sub')), may hold values from 0 to 31
- send_slot: int32 [4096, 2, 9, 2], P(('group', 'sub')), may hold values from 0 to 127, as said below
- recv_block: int32 [16384], P(('group', 'sub')), may hold values from 0 to 32
Outputs:
- coarse: float32 [4096, 128, 128], P(('group', 'sub'))
The draws below stay inside these ranges and needn't reach their ends.
Inputs may be any that keep to these rules, and one draw needn't show every extreme that they name: `a_cols`: values below 32 name the device's own rows, the next 8 the rows received from the previous subdomain, the last 8 those from the next subdomain. `halo_send`: local rows of the sending device; its first 8 entries are for the previous subdomain, the others for the next. `send_slot`: a device number g * 32 + t of any group g, whose sub index t differs from the sending device's sub index by at most 2. `recv_block`: the value 32 means that the sender's partial block is not used.
All inputs are finite; a program needn't handle non-finite values.
Results may differ from the reference program's by a relative error of at most 0.0029.
Values may be sent and summed in bfloat16 or wider, within the bound.
A program may use at most 128 MiB of HBM per device.

```python
import jax
import jax.numpy as jnp
from jax import lax

B = 128
K = 9
KP = 2
ROWS_DEV = 32
OWN = 32
HALO = 8
FINE = 4096
N_GROUP = 4
N_SUB = 32
DEVICES = 128


def draw_send_slot(key, part):
    key = jax.random.fold_in(key, 7)
    key_offset, key_group = jax.random.split(key)
    shape = (FINE, KP, K, KP)
    sender_sub = jnp.arange(FINE) // ROWS_DEV % N_SUB
    offsets = jax.random.randint(key_offset, shape, -2, 3)
    target_sub = jnp.clip(sender_sub[:, None, None, None] + offsets, 0, N_SUB - 1)
    target_group = jax.random.randint(key_group, shape, 0, N_GROUP)
    return (target_group * N_SUB + target_sub).astype(jnp.int32)


def plant(drawn, stream_key, smallest, high):
    longest = drawn.shape.index(max(drawn.shape))
    spots = []
    for shift in (0, 1):
        where = [jax.random.randint(jax.random.fold_in(stream_key, axis), (), 0, length) for axis, length in enumerate(drawn.shape)]
        where[longest] = (where[longest] + shift) % drawn.shape[longest]
        spots.append(tuple(where))
    return drawn.at[spots[0]].set(smallest).at[spots[1]].set(high)


def block_scale(stream_key, shape, cuts, low, largest):
    gain = 1.0
    for axis_at, parts in cuts:
        draws = jax.random.uniform(jax.random.fold_in(jax.random.fold_in(stream_key, 6), axis_at), (parts,), jnp.float32, low / len(cuts), largest / len(cuts))
        gain = gain * jnp.repeat(jnp.exp(draws), shape[axis_at] // parts).reshape((-1,) + (1,) * (len(shape) - 1 - axis_at))
    return gain


def bell_draw(key, shape, spread, limit, pieces=(), kind=jnp.bfloat16):
    array = jax.random.normal(key, shape, jnp.float32) * spread
    if len(pieces) > 0:
        array = block_scale(key, shape, pieces, -0.22, 0.18) * array
    return jnp.clip(array, min=-limit, max=limit).astype(kind)


def setup_inputs(seed: int = 0) -> dict:
    seeds = jax.random.split(jax.random.key(seed), 7)
    return {
        "a_vals": bell_draw(seeds[0], (FINE, K, B, B), B ** -0.5, 0.5, ((0, 128),)),
        "a_cols": plant(jax.random.randint(seeds[1], (FINE, K), 0, ROWS_DEV + 2 * HALO), jax.random.fold_in(seeds[1], 1), 0, (ROWS_DEV + 2 * HALO) - 1).astype(jnp.int32),
        "p_vals": bell_draw(seeds[2], (FINE, KP, B, B), B ** -0.5, 0.5, ((0, 128),)),
        "halo_send": plant(jax.random.randint(seeds[3], (DEVICES * 2 * HALO,), 0, ROWS_DEV), jax.random.fold_in(seeds[3], 1), 0, ROWS_DEV - 1).astype(jnp.int32),
        "send_slot": draw_send_slot(jax.random.fold_in(seeds[6], 71), 0),
        "recv_block": plant(jax.random.randint(seeds[5], (DEVICES * DEVICES,), 0, OWN + 1), jax.random.fold_in(seeds[5], 1), 0, OWN).astype(jnp.int32),
    }


def pick_rows(table, chosen):
    return jnp.take(table, chosen, axis=0)


def reference(a_vals, a_cols, p_vals, halo_send, send_slot, recv_block):
    devices = N_GROUP * N_SUB
    a_all = a_vals.reshape(devices, ROWS_DEV, K, B, B)
    cols_all = a_cols.reshape(devices, ROWS_DEV, K)
    p_all = p_vals.reshape(devices, ROWS_DEV, KP, B, B)
    send_lists = halo_send.reshape(devices, 2 * HALO)
    slot_all = send_slot.reshape(devices, ROWS_DEV, KP, K, KP)
    targets = recv_block.reshape(devices, devices)
    packed = jax.vmap(pick_rows)(p_all, send_lists)
    position = jnp.arange(devices) % N_SUB
    zero_rows = jnp.zeros_like(packed[:1, :HALO])
    from_left = jnp.concatenate([zero_rows, packed[:-1, HALO:]], axis=0)
    from_left = jnp.where((position > 0)[:, None, None, None, None], from_left, jnp.zeros_like(from_left))
    from_right = jnp.concatenate([packed[1:, :HALO], zero_rows], axis=0)
    from_right = jnp.where((position < N_SUB - 1)[:, None, None, None, None], from_right, jnp.zeros_like(from_right))
    extended = jnp.concatenate([p_all, from_left, from_right], axis=1)

    def source(coarse_sum, sender):
        far_rows = jnp.take(extended[sender], cols_all[sender], axis=0)
        product = jnp.einsum("rkuv,rkqvy->rkquy", a_all[sender].astype(jnp.float32), far_rows.astype(jnp.float32))
        product = product.astype(jnp.bfloat16)
        term_blocks = jnp.einsum("rpux,rkquy->rpkqxy", p_all[sender].astype(jnp.float32), product.astype(jnp.float32))
        slot_sums = jnp.zeros((devices, B, B), jnp.float32)
        slot_sums = slot_sums.at[slot_all[sender].reshape(-1)].add(term_blocks.reshape(-1, B, B))
        chosen = targets[:, sender]
        where_to = jnp.where(chosen < OWN, jnp.arange(devices).astype(jnp.int32) * OWN + chosen, devices * OWN)
        return coarse_sum.at[where_to].add(slot_sums), None

    start_sum = jnp.zeros((devices * OWN + 1, B, B), jnp.float32)
    coarse_sum, _ = lax.scan(source, start_sum, jnp.arange(devices).astype(jnp.int32))
    return coarse_sum[:devices * OWN]
```

```python
import functools

import jax
import jax.numpy as jnp
from jax import lax
from jax.experimental import pallas as pl
from jax.experimental.pallas import tpu as pltpu
from jax.sharding import PartitionSpec as P

B = 128
ROWS = 32
SLOTS_A = 9
SLOTS_P = 2
HALO = 8
OWN = 32
N_GROUP = 4
N_SUB = 32
ENTRIES = ROWS * SLOTS_A
WIN = 5
BUCKETS = N_GROUP * WIN
E = 16
RING = 4
U = 8
G = 8
LIST = ENTRIES * 4 + U
DUMMY = ENTRIES * SLOTS_P
RUNS = ENTRIES * 4 // U + BUCKETS + G
MIB = 2**20
MESH = pl.DeviceIdType.MESH
BF = jnp.bfloat16
F32 = jnp.float32
ANY = pl.BlockSpec(memory_space=pl.ANY)
SMEM = pl.BlockSpec(memory_space=pltpu.SMEM)
VMEM = pl.BlockSpec(memory_space=pltpu.VMEM)


def dot(a, b):
    return jnp.dot(a, b, preferred_element_type=F32)


def pack_kernel(halo_send, p_hbm, to_prev, to_next, sems):
    copies = []
    for j in range(2 * HALO):
        out = (to_prev if j < HALO else to_next).at[j % HALO]
        copies.append(pltpu.make_async_copy(p_hbm.at[halo_send[j]], out, sems.at[j]))
    for copy in copies:
        copy.start()
    for copy in copies:
        copy.wait()


def pack_halo(halo_send, p_vals):
    shape = jax.ShapeDtypeStruct((HALO, SLOTS_P, B, B), BF)
    return pl.pallas_call(
        pack_kernel,
        out_shape=(shape, shape),
        in_specs=[SMEM, ANY],
        out_specs=(ANY, ANY),
        scratch_shapes=[pltpu.SemaphoreType.DMA((2 * HALO,))],
        name="pack_halo",
    )(halo_send, p_vals)


def triple(cols, slots, a_hbm, far, p_t, lists, out, a_v, prod, run, entry_list, term_list, count, last, sems, local, init):
    def fetch_all(group, start):
        place = lax.rem(group, RING)
        for u in range(E):
            copy = pltpu.make_async_copy(a_hbm.at[entry_list[group * E + u]], a_v.at[place, u], sems.at[place])
            copy.start()

    def wait_all(group):
        place = lax.rem(group, RING)
        pltpu.make_async_copy(a_hbm.at[pl.ds(0, E)], a_v.at[place], sems.at[place]).wait()

    def list_body(e, n):
        entry_list[n] = e
        return n + ((cols[e] < ROWS) == local).astype(jnp.int32)

    n_entries = lax.fori_loop(0, ENTRIES, list_body, 0, unroll=8)
    for u in range(E):
        entry_list[n_entries + u] = 0
    groups = (n_entries + E - 1) // E
    for g in range(RING):
        pl.when(g < groups)(functools.partial(fetch_all, g, None))
    for s in range(BUCKETS + 1):
        count[s] = 0
    for u in range(U):
        term_list[BUCKETS, u] = DUMMY
    prod[DUMMY] = jnp.zeros((B, B), BF)
    init()

    @pl.loop(0, groups)
    def _(group):
        wait_all(group)
        place = lax.rem(group, RING)
        for u in range(E):
            j = group * E + u
            e = entry_list[j]
            c = cols[e]
            x = far(c)
            x = jnp.concatenate([x[0], x[1]], axis=1)
            y = dot(a_v[place, u], x).astype(BF)
            prod[j * 2] = y[:, :B]
            prod[j * 2 + 1] = y[:, B:]
        for u in range(E):
            j = group * E + u
            e = entry_list[j]
            i = e // SLOTS_A
            k = e - i * SLOTS_A
            step = (j < n_entries).astype(jnp.int32)
            for p in range(SLOTS_P):
                for q in range(SLOTS_P):
                    s = slots[i * 36 + k * 2 + (p * 18 + q)]
                    n = count[s]
                    term_list[s, n] = (i * 2 + p) * 1024 + (j * 2 + q)
                    count[s] = n + step

        @pl.when(group + RING < groups)
        def _():
            fetch_all(group + RING, None)

    chunks = 0
    for s in range(BUCKETS):
        n = count[s]
        for u in range(U):
            term_list[s, n + u] = DUMMY
        chunks = chunks + jnp.maximum((n + U - 1) // U, 1)

    def step_body(it, carry):
        s, off, acc = carry
        for g in range(G):
            left, right = [], []
            for u in range(U):
                w = term_list[s, off + u]
                left.append(p_t[w >> 10])
                right.append(prod[w & 1023])
            keep = (off > 0).astype(F32)
            acc = acc * keep + dot(jnp.concatenate(left, axis=1), jnp.concatenate(right, axis=0))
            j = it * G + g
            run[j] = acc
            last[s] = j
            off = off + U
            done = off >= count[s]
            off = jnp.where(done, 0, off)
            s = jnp.where(done, jnp.minimum(s + 1, BUCKETS), s)
        return s, off, acc

    lax.fori_loop(0, (chunks + G - 1) // G, step_body, (0, 0, jnp.zeros((B, B), F32)))


def local_kernel(cols, slots, a_hbm, p_hbm, out, pt_out, a_v, p_v, p_t, prod, run, entry_list, term_list, count, last, sems, p_sem, pt_sem):
    load = pltpu.make_async_copy(p_hbm, p_v, p_sem)
    load.start()
    save = pltpu.make_async_copy(p_t, pt_out, pt_sem)

    def init():
        load.wait()

        @pl.loop(0, ROWS)
        def _(i):
            for p in range(SLOTS_P):
                p_t[i * 2 + p] = p_v[i, p].T

        save.start()

    triple(cols, slots, a_hbm, lambda c: p_v[jnp.minimum(c, ROWS - 1)], p_t, None, out, a_v, prod, run, entry_list, term_list, count, last, sems, True, init)
    for s in range(BUCKETS):
        out[s] = run[last[s]]
    save.wait()


def far_kernel(cols, slots, a_hbm, pt_hbm, before, after, acc, out, a_v, h_v, p_t, prod, run, entry_list, term_list, count, last, sems, in_sems):
    loads = [
        pltpu.make_async_copy(before, h_v.at[pl.ds(0, HALO)], in_sems.at[0]),
        pltpu.make_async_copy(after, h_v.at[pl.ds(HALO, HALO)], in_sems.at[1]),
        pltpu.make_async_copy(pt_hbm, p_t, in_sems.at[2]),
    ]
    for load in loads:
        load.start()

    def init():
        for load in loads:
            load.wait()

    triple(cols, slots, a_hbm, lambda c: h_v[jnp.maximum(c - ROWS, 0)], p_t, None, out, a_v, prod, run, entry_list, term_list, count, last, sems, False, init)
    for s in range(BUCKETS):
        out[s] = (acc[s] + run[last[s]]).astype(BF)


def common_scratch():
    return [
        pltpu.VMEM((ENTRIES * 2 + 2 * E + 8, B, B), BF),
        pltpu.VMEM((RUNS, B, B), F32),
        pltpu.SMEM((ENTRIES + E,), jnp.int32),
        pltpu.SMEM((BUCKETS + 1, LIST), jnp.int32),
        pltpu.SMEM((BUCKETS + 1,), jnp.int32),
        pltpu.SMEM((BUCKETS + 1,), jnp.int32),
        pltpu.SemaphoreType.DMA((RING,)),
    ]


def local_terms(cols, slots, a, p_vals):
    return pl.pallas_call(
        local_kernel,
        out_shape=(jax.ShapeDtypeStruct((BUCKETS, B, B), F32), jax.ShapeDtypeStruct((ROWS * 2, B, B), BF)),
        in_specs=[SMEM, SMEM, ANY, ANY],
        out_specs=(VMEM, ANY),
        scratch_shapes=[
            pltpu.VMEM((RING, E, B, B), BF),
            pltpu.VMEM((ROWS, SLOTS_P, B, B), BF),
            pltpu.VMEM((ROWS * 2, B, B), BF),
        ]
        + common_scratch()
        + [pltpu.SemaphoreType.DMA, pltpu.SemaphoreType.DMA],
        compiler_params=pltpu.CompilerParams(vmem_limit_bytes=56 * MIB),
        cost_estimate=pl.CostEstimate(flops=6 * 10**9, bytes_accessed=30 * 10**6, transcendentals=0),
        name="local_terms",
    )(cols, slots, a, p_vals)


def far_terms(cols, slots, a, p_t, before, after, acc):
    return pl.pallas_call(
        far_kernel,
        out_shape=jax.ShapeDtypeStruct((BUCKETS, B, B), BF),
        in_specs=[SMEM, SMEM, ANY, ANY, ANY, ANY, VMEM],
        out_specs=VMEM,
        scratch_shapes=[
            pltpu.VMEM((RING, E, B, B), BF),
            pltpu.VMEM((2 * HALO, SLOTS_P, B, B), BF),
            pltpu.VMEM((ROWS * 2, B, B), BF),
        ]
        + common_scratch()
        + [pltpu.SemaphoreType.DMA((3,))],
        compiler_params=pltpu.CompilerParams(vmem_limit_bytes=56 * MIB),
        name="far_terms",
    )(cols, slots, a, p_t, before, after, acc)


def exchange_kernel(partial, received, send_sems, recv_sems, own_sem):
    g = lax.axis_index("group")
    s = lax.axis_index("sub")
    peers = []
    for dg in (2, 1, 3, 0):
        for off in range(-2, 3):
            if dg or off:
                peers.append((dg, off, lax.rem(g + dg, N_GROUP), lax.rem(s + (off + N_SUB), N_SUB)))
    barrier = pltpu.get_barrier_semaphore()
    for _, _, tg, ts in peers:
        pl.semaphore_signal(barrier, inc=1, device_id=(tg, ts), device_id_type=MESH)
    own = pltpu.make_async_copy(partial.at[g * WIN + 2], received.at[2], own_sem)
    own.start()
    pl.semaphore_wait(barrier, len(peers))
    copies = []
    for dg, off, tg, ts in peers:
        j = dg * WIN + off + 2
        copy = pltpu.make_async_remote_copy(
            src_ref=partial.at[tg * WIN + (off + 2)],
            dst_ref=received.at[j],
            send_sem=send_sems.at[j],
            recv_sem=recv_sems.at[j],
            device_id=(tg, ts),
            device_id_type=MESH,
        )
        copy.start()
        copies.append(copy)
    own.wait()
    for copy in copies:
        copy.wait()


def exchange(partial):
    return pl.pallas_call(
        exchange_kernel,
        out_shape=jax.ShapeDtypeStruct((BUCKETS, B, B), BF),
        in_specs=[ANY],
        out_specs=ANY,
        scratch_shapes=[
            pltpu.SemaphoreType.DMA((BUCKETS,)),
            pltpu.SemaphoreType.DMA((BUCKETS,)),
            pltpu.SemaphoreType.DMA,
        ],
        compiler_params=pltpu.CompilerParams(collective_id=0, has_side_effects=True),
        name="exchange",
    )(partial)


def place_kernel(targets, received, out):
    g = lax.axis_index("group")
    s = lax.axis_index("sub")
    out[...] = jnp.zeros_like(out)
    for dg in range(N_GROUP):
        for off in range(-2, 3):
            sg = lax.rem(g - dg + N_GROUP, N_GROUP)
            ss = s - off
            inside = jnp.logical_and(ss >= 0, ss < N_SUB)
            o = targets[jnp.where(inside, sg * N_SUB + ss, 0)]

            @pl.when(jnp.logical_and(inside, o < OWN))
            def _():
                out[o] += received[dg * WIN + off + 2].astype(F32)


def place(targets, received):
    return pl.pallas_call(
        place_kernel,
        out_shape=jax.ShapeDtypeStruct((OWN, B, B), F32),
        in_specs=[SMEM, VMEM],
        out_specs=VMEM,
        name="place",
    )(targets, received)


def per_device(a_vals, a_cols, p_vals, halo_send, send_slot, recv_block):
    my_sub = lax.axis_index("sub")
    to_prev, to_next = pack_halo(halo_send, p_vals)
    up = [(i, i + 1) for i in range(N_SUB - 1)]
    down = [(j, i) for i, j in up]
    before = lax.ppermute(to_next, "sub", up)
    after = lax.ppermute(to_prev, "sub", down)
    cols = a_cols.reshape(-1)
    flat = send_slot.reshape(-1)
    slots = flat // N_SUB * WIN + (flat % N_SUB - my_sub + 2)
    a = a_vals.reshape(ENTRIES, B, B)
    acc, p_t = local_terms(cols, slots, a, p_vals)
    partial = far_terms(cols, slots, a, p_t, before, after, acc)
    received = exchange(partial)
    return place(recv_block, received)


def solution(mesh):
    return jax.shard_map(
        per_device,
        mesh=mesh,
        in_specs=(
            P(("group", "sub"), None, None, None),
            P(("group", "sub"), None),
            P(("group", "sub"), None, None, None),
            P(("group", "sub")),
            P(("group", "sub"), None, None, None),
            P(("group", "sub")),
        ),
        out_specs=P(("group", "sub"), None, None),
        check_vma=False,
    )
```

```python
import functools

import jax
import jax.numpy as jnp
from jax import lax
from jax.experimental import pallas as pl
from jax.experimental.pallas import tpu as pltpu
from jax.sharding import PartitionSpec as P

B = 128
ROWS = 32
SLOTS_A = 9
SLOTS_P = 2
HALO = 8
OWN = 32
N_GROUP = 4
N_SUB = 32
ENTRIES = ROWS * SLOTS_A
TERMS = ENTRIES * 4
WIN = 5
BUCKETS = N_GROUP * WIN
ROW_RING = 8
ROW_STEP = 2
E = 16
RING = 4
U = 8
G = 8
CHUNKS = 168
PRODS = 2 * ENTRIES + 8
WORD_ROWS = 16
TABLE_ROWS = 24
MIB = 2**20
MESH = pl.DeviceIdType.MESH
BF = jnp.bfloat16
F32 = jnp.float32
SMEM = pl.BlockSpec(memory_space=pltpu.SMEM)
VMEM = pl.BlockSpec(memory_space=pltpu.VMEM)
HBM = pl.BlockSpec(memory_space=pltpu.HBM)


def in_hbm(x):
    return pltpu.with_memory_space_constraint(x, pltpu.HBM)


def in_vmem(x):
    return pltpu.with_memory_space_constraint(x, pltpu.VMEM)


def dot(a, b):
    return jnp.dot(a, b, preferred_element_type=F32)


def product(a, x):
    return dot(a, jnp.concatenate([x[0], x[1]], axis=1)).astype(BF)


def own_kernel(cols, halo_send, a_hbm, p_hbm, prods, p_t, halo, a_v, p_v, packed, a_sems, p_sem, send_sems, recv_sems):
    g = lax.axis_index("group")
    s = lax.axis_index("sub")
    before = (g, lax.rem(s + (N_SUB - 1), N_SUB))
    after = (g, lax.rem(s + 1, N_SUB))
    barrier = pltpu.get_barrier_semaphore()
    for peer in (before, after):
        pl.semaphore_signal(barrier, inc=1, device_id=peer, device_id_type=MESH)
    load = pltpu.make_async_copy(p_hbm, p_v, p_sem)
    load.start()

    def fetch(i):
        place = lax.rem(i, ROW_RING)
        return pltpu.make_async_copy(a_hbm.at[i], a_v.at[place], a_sems.at[place])

    for i in range(ROW_RING):
        fetch(i).start()
    load.wait()
    for j in range(2 * HALO):
        packed[j] = p_v[halo_send[j]]
    pl.semaphore_wait(barrier, 2)
    copies = [
        pltpu.make_async_remote_copy(
            src_ref=packed.at[pl.ds(src, HALO)],
            dst_ref=halo.at[pl.ds(HALO - src, HALO)],
            send_sem=send_sems.at[n],
            recv_sem=recv_sems.at[n],
            device_id=peer,
            device_id_type=MESH,
        )
        for n, (src, peer) in enumerate(((0, before), (HALO, after)))
    ]
    for copy in copies:
        copy.start()
    for j in range(2):
        prods[j] = jnp.zeros((B, B), BF)

    @pl.loop(0, ROWS // ROW_STEP)
    def _(step):
        for r in range(ROW_STEP):
            fetch(step * ROW_STEP + r).wait()
        for r in range(ROW_STEP):
            i = step * ROW_STEP + r
            place = lax.rem(i, ROW_RING)
            for k in range(SLOTS_A):
                e = i * SLOTS_A + k
                y = product(a_v[place, k], p_v[jnp.minimum(cols[e], ROWS - 1)])
                prods[e * 2 + 2] = y[:, :B]
                prods[e * 2 + 3] = y[:, B:]
            for p in range(SLOTS_P):
                p_t[i * 2 + p] = p_v[i, p].T
        for r in range(ROW_STEP):
            i = step * ROW_STEP + r + ROW_RING

            @pl.when(i < ROWS)
            def _():
                fetch(i).start()

    for copy in copies:
        copy.wait()

    @pl.when(s == 0)
    def _():
        halo[pl.ds(0, HALO)] = jnp.zeros((HALO, SLOTS_P, B, B), BF)

    @pl.when(s == N_SUB - 1)
    def _():
        halo[pl.ds(HALO, HALO)] = jnp.zeros((HALO, SLOTS_P, B, B), BF)


def own_products(cols, halo_send, a_vals, p_vals):
    return pl.pallas_call(
        own_kernel,
        out_shape=(
            pltpu.VMEM((PRODS, B, B), BF),
            pltpu.VMEM((2 * ROWS, B, B), BF),
            pltpu.VMEM((2 * HALO, SLOTS_P, B, B), BF),
        ),
        in_specs=[SMEM, SMEM, HBM, HBM],
        out_specs=(VMEM, VMEM, VMEM),
        scratch_shapes=[
            pltpu.VMEM((ROW_RING, SLOTS_A, B, B), BF),
            pltpu.VMEM((ROWS, SLOTS_P, B, B), BF),
            pltpu.VMEM((2 * HALO, SLOTS_P, B, B), BF),
            pltpu.SemaphoreType.DMA((ROW_RING,)),
            pltpu.SemaphoreType.DMA,
            pltpu.SemaphoreType.DMA((2,)),
            pltpu.SemaphoreType.DMA((2,)),
        ],
        compiler_params=pltpu.CompilerParams(collective_id=0, has_side_effects=True, vmem_limit_bytes=8 * MIB),
        name="own_products",
    )(cols, halo_send, in_hbm(a_vals), in_hbm(p_vals))


def iota(shape, axis):
    return lax.broadcasted_iota(jnp.int32, shape, axis)


def build_table(slots, table):
    rows = TERMS // B
    width = 32
    one_hot = [
        (jnp.broadcast_to(slots[r : r + 1, :], (width, B)) == iota((width, B), 0)).astype(F32) for r in range(rows)
    ]
    stacked = jnp.concatenate(one_hot, axis=0).astype(BF)
    upper = (iota((B, B), 0) < iota((B, B), 1)).astype(F32).astype(BF)
    rank = dot(stacked, upper)
    total = dot(stacked, jnp.ones((B, B), BF))
    base = jnp.zeros((width, B), F32)
    ranks = []
    for r in range(rows):
        ranks.append(base + rank[r * width : (r + 1) * width])
        base = base + total[r * width : (r + 1) * width]
    bucket = iota((width, B), 0)
    used = ((base.astype(jnp.int32) + (U - 1)) >> 3).astype(F32)
    used = jnp.where(bucket < BUCKETS, jnp.maximum(used, 1.0), 0.0)
    lower = (iota((width, width), 1) < iota((width, width), 0)).astype(F32).astype(BF)
    first = dot(lower, used.astype(BF))
    words = jnp.zeros((3 * WORD_ROWS, B), F32)
    lane = iota((1, B), 1)
    for r in range(rows):
        pos = jnp.sum(one_hot[r] * (first * float(U) + ranks[r]), axis=0, keepdims=True).astype(jnp.int32)
        term = lane + r * B
        i = (term * 1821) >> 16
        rest = term - i * 36
        p = (rest >= 18).astype(jnp.int32)
        block = i * 18 + (rest - p * 18) + 2
        here = jnp.broadcast_to(pos >> 7, (WORD_ROWS, B)) == iota((WORD_ROWS, B), 0)
        parts = [
            jnp.where(here, jnp.broadcast_to(v.astype(F32), (WORD_ROWS, B)), 0.0)
            for v in (i * 2 + p, block >> 4, block & 15)
        ]
        low = (jnp.broadcast_to(pos & (B - 1), (B, B)) == iota((B, B), 0)).astype(F32).astype(BF)
        words = words + lax.dot_general(
            jnp.concatenate(parts, axis=0).astype(BF),
            low,
            (((1,), (1,)), ((), ())),
            preferred_element_type=F32,
        )
    words = words.astype(jnp.int32)
    table[0:WORD_ROWS, :] = words[:WORD_ROWS] * 1024 + words[WORD_ROWS : 2 * WORD_ROWS] * 16 + words[2 * WORD_ROWS :]
    lane32 = iota((width, B), 1).astype(F32)
    starts = jnp.where(bucket < BUCKETS, first, -1.0)
    keep = [1.0 - jnp.sum((starts == lane32 + float(h * B)).astype(F32), axis=0, keepdims=True) for h in range(2)]
    last = jnp.sum(jnp.where(bucket == iota((width, B), 1), first + used - 1.0, 0.0), axis=0, keepdims=True)
    rest = jnp.concatenate(keep + [last, jnp.zeros((5, B), F32)], axis=0)
    table[WORD_ROWS:TABLE_ROWS, :] = rest.astype(jnp.int32)


def far_kernel(cols, slots, a_hbm, halo, _, prods, table, a_v, entry_list, a_sems):
    def fetch(group):
        place = lax.rem(group, RING)
        for u in range(E):
            pltpu.make_async_copy(a_hbm.at[entry_list[group * E + u]], a_v.at[place, u], a_sems.at[place]).start()

    def fetched(group):
        place = lax.rem(group, RING)
        pltpu.make_async_copy(a_hbm.at[pl.ds(0, E)], a_v.at[place], a_sems.at[place]).wait()

    def list_body(e, n):
        entry_list[n] = e
        return n + (cols[e] >= ROWS).astype(jnp.int32)

    entries = lax.fori_loop(0, ENTRIES, list_body, 0, unroll=16)
    groups = (entries + (E - 1)) // E

    @pl.when(entries > 0)
    def _():
        tail = entry_list[entries - 1]
        for u in range(E):
            entry_list[entries + u] = tail

    for group in range(RING):
        pl.when(group < groups)(functools.partial(fetch, group))
    build_table(slots, table)

    @pl.loop(0, groups)
    def _(group):
        place = lax.rem(group, RING)
        fetched(group)

        for u in range(E):
            e = entry_list[group * E + u]
            y = product(a_v[place, u], halo[cols[e] - ROWS])
            prods[e * 2 + 2] = y[:, :B]
            prods[e * 2 + 3] = y[:, B:]

        @pl.when(group + RING < groups)
        def _():
            fetch(group + RING)


def far_products(cols, slots, a, halo, prods):
    return pl.pallas_call(
        far_kernel,
        out_shape=(
            pltpu.VMEM((PRODS, B, B), BF),
            jax.ShapeDtypeStruct((TABLE_ROWS, B), jnp.int32),
        ),
        in_specs=[SMEM, VMEM, HBM, VMEM, VMEM],
        out_specs=(VMEM, VMEM),
        scratch_shapes=[
            pltpu.VMEM((RING, E, B, B), BF),
            pltpu.SMEM((ENTRIES + E,), jnp.int32),
            pltpu.SemaphoreType.DMA((RING,)),
        ],
        input_output_aliases={4: 0},
        compiler_params=pltpu.CompilerParams(vmem_limit_bytes=12 * MIB),
        name="far_products",
    )(cols, slots, in_hbm(a), in_vmem(halo), in_vmem(prods))


def term_kernel(table, prods, p_t, received, run, partial, send_sems, recv_sems):
    g = lax.axis_index("group")
    s = lax.axis_index("sub")
    peers = []
    for dg in (2, 1, 3, 0):
        for off in range(-2, 3):
            if dg or off:
                peers.append((dg, off, lax.rem(g + dg, N_GROUP), lax.rem(s + (off + N_SUB), N_SUB)))
    barrier = pltpu.get_barrier_semaphore()
    for _, _, tg, ts in peers:
        pl.semaphore_signal(barrier, inc=1, device_id=(tg, ts), device_id_type=MESH)

    def step(it, acc):
        for n in range(G):
            c = it * G + n
            left, right = [], []
            for u in range(U):
                w = table[c * U + u]
                left.append(p_t[w >> 10])
                right.append(prods[w & 1023])
            keep = table[WORD_ROWS * B + c].astype(F32)
            acc = acc * keep + dot(jnp.concatenate(left, axis=1), jnp.concatenate(right, axis=0))
            run[c] = acc
        return acc

    lax.fori_loop(0, CHUNKS // G, step, jnp.zeros((B, B), F32))
    pl.semaphore_wait(barrier, len(peers))
    copies = []
    for dg, off, tg, ts in peers:
        j = dg * WIN + off + 2
        partial[j] = run[table[(WORD_ROWS + 2) * B + tg * WIN + (off + 2)]].astype(BF)
        copy = pltpu.make_async_remote_copy(
            src_ref=partial.at[j],
            dst_ref=received.at[j],
            send_sem=send_sems.at[j],
            recv_sem=recv_sems.at[j],
            device_id=(tg, ts),
            device_id_type=MESH,
        )
        copy.start()
        copies.append(copy)
    received[2] = run[table[(WORD_ROWS + 2) * B + g * WIN + 2]].astype(BF)
    for copy in copies:
        copy.wait()


def send_terms(table, prods, p_t):
    return pl.pallas_call(
        term_kernel,
        out_shape=jax.ShapeDtypeStruct((BUCKETS, B, B), BF),
        in_specs=[SMEM, VMEM, VMEM],
        out_specs=VMEM,
        scratch_shapes=[
            pltpu.VMEM((CHUNKS, B, B), F32),
            pltpu.VMEM((BUCKETS, B, B), BF),
            pltpu.SemaphoreType.DMA((BUCKETS,)),
            pltpu.SemaphoreType.DMA((BUCKETS,)),
        ],
        compiler_params=pltpu.CompilerParams(collective_id=1, has_side_effects=True, vmem_limit_bytes=16 * MIB),
        name="send_terms",
    )(table, in_vmem(prods), in_vmem(p_t))


def place_kernel(targets, received, out):
    g = lax.axis_index("group")
    s = lax.axis_index("sub")
    out[...] = jnp.zeros_like(out)
    for dg in range(N_GROUP):
        for off in range(-2, 3):
            sg = lax.rem(g - dg + N_GROUP, N_GROUP)
            ss = s - off
            inside = jnp.logical_and(ss >= 0, ss < N_SUB)
            o = targets[jnp.where(inside, sg * N_SUB + ss, 0)]

            @pl.when(jnp.logical_and(inside, o < OWN))
            def _():
                out[o] += received[dg * WIN + off + 2].astype(F32)


def place(targets, received):
    return pl.pallas_call(
        place_kernel,
        out_shape=jax.ShapeDtypeStruct((OWN, B, B), F32),
        in_specs=[SMEM, VMEM],
        out_specs=VMEM,
        name="place",
    )(targets, in_vmem(received))


def per_device(a_vals, a_cols, p_vals, halo_send, send_slot, recv_block):
    my_sub = lax.axis_index("sub")
    cols = a_cols.reshape(-1)
    prods, p_t, halo = own_products(cols, halo_send, a_vals, p_vals)
    flat = send_slot.reshape(TERMS // B, B)
    slots = flat // N_SUB * WIN + (flat % N_SUB - my_sub + 2)
    prods, table = far_products(cols, slots, a_vals.reshape(ENTRIES, B, B), halo, prods)
    received = send_terms(table.reshape(-1), prods, p_t)
    return place(recv_block, received)


def solution(mesh):
    return jax.shard_map(
        per_device,
        mesh=mesh,
        in_specs=(
            P(("group", "sub"), None, None, None),
            P(("group", "sub"), None),
            P(("group", "sub"), None, None, None),
            P(("group", "sub")),
            P(("group", "sub"), None, None, None),
            P(("group", "sub")),
        ),
        out_specs=P(("group", "sub"), None, None),
        check_vma=False,
    )
```

```python
import functools

import jax
import jax.numpy as jnp
from jax import lax
from jax.experimental import pallas as pl
from jax.experimental.pallas import tpu as pltpu
from jax.sharding import PartitionSpec as P

B = 128
ROWS = 32
SLOTS_A = 9
SLOTS_P = 2
HALO = 8
OWN = 32
N_GROUP = 4
N_SUB = 32
ENTRIES = ROWS * SLOTS_A
TERMS = ENTRIES * 4
WIN = 5
BUCKETS = N_GROUP * WIN
ROW_RING = 16
ROW_STEP = 4
U = 4
G = 77
CHUNKS = 308
LEFTS = 2 * ENTRIES + 8
OWN_BLOCKS = ROWS * SLOTS_P
FAR_BLOCKS = 2 * HALO * SLOTS_P
WIDTH = 32
WORD_ROWS = 16
KEEP_ROWS = 3
TABLE_ROWS = 24
CODE = 32767.0
MIB = 2**20
MESH = pl.DeviceIdType.MESH
BF = jnp.bfloat16
F32 = jnp.float32
I16 = jnp.int16
SMEM = pl.BlockSpec(memory_space=pltpu.SMEM)
VMEM = pl.BlockSpec(memory_space=pltpu.VMEM)
HBM = pl.BlockSpec(memory_space=pltpu.HBM)


def in_hbm(x):
    return pltpu.with_memory_space_constraint(x, pltpu.HBM)


def in_vmem(x):
    return pltpu.with_memory_space_constraint(x, pltpu.VMEM)


def dot(a, b):
    return jnp.dot(a, b, preferred_element_type=F32)


def group_at(g, d):
    return g + (d % 2) * jnp.where(lax.rem(g, 2) == 0, 1, -1) + (d // 2) * jnp.where(g < 2, 2, -2)


def iota(shape, axis):
    return lax.broadcasted_iota(jnp.int32, shape, axis)


def build_table(my_sub, cols, slots, table):
    slot = jnp.concatenate([slots[p, :, q, :] for p in range(SLOTS_P) for q in range(SLOTS_P)], axis=1)
    bucket_of = (slot >> 5) * WIN + ((slot & (N_SUB - 1)) - my_sub + 2)
    col = jnp.concatenate([cols[...]] * 4, axis=1)
    rows = SLOTS_A
    one_hot = [
        (jnp.broadcast_to(bucket_of[r : r + 1, :], (WIDTH, B)) == iota((WIDTH, B), 0)).astype(F32) for r in range(rows)
    ]
    stacked = jnp.concatenate(one_hot, axis=0).astype(BF)
    upper = (iota((B, B), 0) < iota((B, B), 1)).astype(F32).astype(BF)
    rank = dot(stacked, upper)
    total = dot(stacked, jnp.ones((B, B), BF))
    base = jnp.zeros((WIDTH, B), F32)
    ranks = []
    for r in range(rows):
        ranks.append(base + rank[r * WIDTH : (r + 1) * WIDTH])
        base = base + total[r * WIDTH : (r + 1) * WIDTH]
    bucket = iota((WIDTH, B), 0)
    used = ((base.astype(jnp.int32) + (U - 1)) >> (U.bit_length() - 1)).astype(F32)
    used = jnp.where(bucket < BUCKETS, jnp.maximum(used, 1.0), 0.0)
    lower = (iota((WIDTH, WIDTH), 1) < iota((WIDTH, WIDTH), 0)).astype(F32)
    first = jnp.dot(lower, used, precision=lax.Precision.HIGHEST, preferred_element_type=F32)
    lane = iota((1, B), 1)
    i = lane & (ROWS - 1)
    p = lane >> 6
    q = (lane >> 5) & 1
    words = jnp.zeros((3 * WORD_ROWS, B), F32)
    for r in range(rows):
        pos = jnp.sum(one_hot[r] * (first * float(U) + ranks[r]), axis=0, keepdims=True).astype(jnp.int32)
        left = (i * SLOTS_A + r) * 2 + p + 2
        here = jnp.broadcast_to(pos >> 7, (WORD_ROWS, B)) == iota((WORD_ROWS, B), 0)
        parts = [
            jnp.where(here, jnp.broadcast_to(v.astype(F32), (WORD_ROWS, B)), 0.0)
            for v in (col[r : r + 1, :] * 2 + q, left >> 4, left & 15)
        ]
        low = (jnp.broadcast_to(pos & (B - 1), (B, B)) == iota((B, B), 0)).astype(F32).astype(BF)
        words = words + lax.dot_general(
            jnp.concatenate(parts, axis=0).astype(BF),
            low,
            (((1,), (1,)), ((), ())),
            preferred_element_type=F32,
        )
    words = words.astype(jnp.int32)
    table[0:WORD_ROWS, :] = words[:WORD_ROWS] * 1024 + words[WORD_ROWS : 2 * WORD_ROWS] * 16 + words[2 * WORD_ROWS :]
    starts = jnp.where(bucket < BUCKETS, first, -1.0)
    chunk = iota((WIDTH, B), 1).astype(F32)
    keep = [
        1.0 - jnp.sum((starts == chunk + float(h * B)).astype(F32), axis=0, keepdims=True) for h in range(KEEP_ROWS)
    ]
    last = jnp.sum(jnp.where(bucket == iota((WIDTH, B), 1), first + used - 1.0, 0.0), axis=0, keepdims=True)
    rest = jnp.concatenate(keep + [last, jnp.zeros((7 - KEEP_ROWS, B), F32)], axis=0)
    table[WORD_ROWS:TABLE_ROWS, :] = rest.astype(jnp.int32)


def left_kernel(
    cols_hbm, slots_hbm, send_hbm, a_hbm, p_hbm, lefts, rights, table,
    cols, slots, halo_send, a_v, p_v, packed, a_sems, p_sems, send_sems, recv_sems,
):
    g = lax.axis_index("group")
    s = lax.axis_index("sub")
    sides = ((s > 0, (g, jnp.maximum(s - 1, 0))), (s < N_SUB - 1, (g, jnp.minimum(s + 1, N_SUB - 1))))
    barrier = pltpu.get_barrier_semaphore()
    for there, peer in sides:

        @pl.when(there)
        def _():
            pl.semaphore_signal(barrier, inc=1, device_id=peer, device_id_type=MESH)

    load = pltpu.make_async_copy(p_hbm, p_v, p_sems.at[0])
    keep = pltpu.make_async_copy(p_hbm, rights.at[pl.ds(0, OWN_BLOCKS)], p_sems.at[1])
    small = [
        pltpu.make_async_copy(src, dst, p_sems.at[2 + n])
        for n, (src, dst) in enumerate(((send_hbm, halo_send), (cols_hbm, cols), (slots_hbm, slots)))
    ]
    small[0].start()
    load.start()
    small[1].start()
    small[2].start()

    def fetch(i):
        place = lax.rem(i, ROW_RING)
        return pltpu.make_async_copy(a_hbm.at[i], a_v.at[place], a_sems.at[place])

    for i in range(ROW_RING):
        fetch(i).start()
    keep.start()
    for copy in small:
        copy.wait()
    zero = jnp.zeros((B, B), BF)
    load.wait()
    for j in range(2 * HALO):
        row = halo_send[j]
        for q in range(SLOTS_P):
            packed[j * 2 + q] = p_v[row * 2 + q]
    half = FAR_BLOCKS // 2
    copies = []
    for n, (there, peer) in enumerate(sides):
        copies.append(
            pltpu.make_async_remote_copy(
                src_ref=packed.at[pl.ds(n * half, half)],
                dst_ref=rights.at[pl.ds(OWN_BLOCKS + half - n * half, half)],
                send_sem=send_sems.at[n],
                recv_sem=recv_sems.at[n],
                device_id=peer,
                device_id_type=MESH,
            )
        )
    pl.semaphore_wait(barrier, sum(there.astype(jnp.int32) for there, _ in sides))
    for (there, _), copy in zip(sides, copies):

        @pl.when(there)
        def _():
            copy.start()

    lefts[0] = zero
    lefts[1] = zero
    build_table(s, cols, slots, table)

    @pl.loop(0, ROWS // ROW_STEP)
    def _(step):
        for r in range(ROW_STEP):
            fetch(step * ROW_STEP + r).wait()
        for r in range(ROW_STEP):
            i = step * ROW_STEP + r
            place = lax.rem(i, ROW_RING)
            p_t = jnp.concatenate([p_v[i * 2].T, p_v[i * 2 + 1].T], axis=0)
            first = i * (2 * SLOTS_A) + 2
            for k in range(0, SLOTS_A - 1, 2):
                y = dot(p_t, jnp.concatenate([a_v[place, k], a_v[place, k + 1]], axis=1)).astype(BF)
                for n in range(2):
                    for p in range(SLOTS_P):
                        lefts[first + (k + n) * 2 + p] = y[p * B : (p + 1) * B, n * B : (n + 1) * B]
            k = SLOTS_A - 1
            both = jnp.concatenate([p_t[:B], p_t[B:]], axis=1)
            top = jnp.concatenate([a_v[place, k], zero], axis=1)
            bottom = jnp.concatenate([zero, a_v[place, k]], axis=1)
            y = dot(both, jnp.concatenate([top, bottom], axis=0)).astype(BF)
            for p in range(SLOTS_P):
                lefts[first + k * 2 + p] = y[:, p * B : (p + 1) * B]
        for r in range(ROW_STEP):
            i = step * ROW_STEP + r + ROW_RING

            @pl.when(i < ROWS)
            def _():
                fetch(i).start()

    keep.wait()
    for n, (there, _) in enumerate(sides):

        @pl.when(there)
        def _():
            copies[n].wait_send()
            copies[1 - n].wait_recv()

        @pl.when(jnp.logical_not(there))
        def _():
            rights[pl.ds(OWN_BLOCKS + n * half, half)] = jnp.zeros((half, B, B), BF)


def left_blocks(cols, slots, halo_send, a_vals, p_blocks):
    return pl.pallas_call(
        left_kernel,
        out_shape=(
            pltpu.VMEM((LEFTS, B, B), BF),
            pltpu.VMEM((OWN_BLOCKS + FAR_BLOCKS, B, B), BF),
            jax.ShapeDtypeStruct((TABLE_ROWS, B), jnp.int32),
        ),
        in_specs=[HBM] * 5,
        out_specs=(VMEM, VMEM, VMEM),
        scratch_shapes=[
            pltpu.VMEM((SLOTS_A, ROWS), jnp.int32),
            pltpu.VMEM((SLOTS_P, SLOTS_A, SLOTS_P, ROWS), jnp.int32),
            pltpu.SMEM((2 * HALO,), jnp.int32),
            pltpu.VMEM((ROW_RING, SLOTS_A, B, B), BF),
            pltpu.VMEM((OWN_BLOCKS, B, B), BF),
            pltpu.VMEM((FAR_BLOCKS, B, B), BF),
            pltpu.SemaphoreType.DMA((ROW_RING,)),
            pltpu.SemaphoreType.DMA((5,)),
            pltpu.SemaphoreType.DMA((2,)),
            pltpu.SemaphoreType.DMA((2,)),
        ],
        compiler_params=pltpu.CompilerParams(collective_id=0, has_side_effects=True, vmem_limit_bytes=10 * MIB),
        name="left_blocks",
    )(*[in_hbm(x) for x in (cols, slots, halo_send, a_vals, p_blocks)])


def term_kernel(table, lefts, rights, received, scales, run, coded, scale, sems):
    g = lax.axis_index("group")
    s = lax.axis_index("sub")
    peers = []
    for off in (2, -2, 1, -1, 0):
        for dg in (3, 2, 1, 0):
            if dg or off:
                there = jnp.logical_and(s + off >= 0, s + off < N_SUB)
                ts = jnp.clip(s + off, 0, N_SUB - 1)
                tg = group_at(g, dg)
                peers.append((dg, off, there, tg, ts))
    barrier = pltpu.get_barrier_semaphore()
    for _, _, there, tg, ts in peers:

        @pl.when(there)
        def _():
            pl.semaphore_signal(barrier, inc=1, device_id=(tg, ts), device_id_type=MESH)

    def step(it, acc):
        for n in range(G):
            c = it * G + n
            left, right = [], []
            for u in range(U):
                w = table[c * U + u]
                left.append(lefts[w & 1023])
                right.append(rights[w >> 10])
            keep = table[WORD_ROWS * B + c].astype(F32)
            acc = acc * keep + dot(jnp.concatenate(left, axis=1), jnp.concatenate(right, axis=0))
            run[c] = acc
        return acc

    lax.fori_loop(0, CHUNKS // G, step, jnp.zeros((B, B), F32))

    def code(bucket):
        total = run[table[(WORD_ROWS + KEEP_ROWS) * B + bucket]]
        top = jnp.maximum(jnp.max(jnp.abs(total), axis=0, keepdims=True), 1e-30)
        return jnp.round(total * (CODE / top)).astype(jnp.int32).astype(I16), top * (1.0 / CODE)

    pl.semaphore_wait(barrier, sum(peer[2].astype(jnp.int32) for peer in peers))

    copies = []
    for dg, off, there, tg, ts in peers:
        j = dg * WIN + off + 2
        pair = [
            pltpu.make_async_remote_copy(
                src_ref=src.at[j],
                dst_ref=dst.at[j],
                send_sem=sems.at[2 * n, j],
                recv_sem=sems.at[2 * n + 1, j],
                device_id=(tg, ts),
                device_id_type=MESH,
            )
            for n, (src, dst) in enumerate(((coded, received), (scale, scales)))
        ]
        copies.append(pair)

        @pl.when(there)
        def _():
            coded[j], scale[j] = code(tg * WIN + (off + 2))
            for copy in pair:
                copy.start()

    received[2], scales[2] = code(g * WIN + 2)
    for (dg, off, there, _, _), pair in zip(peers, copies):
        from_there = jnp.logical_and(s - off >= 0, s - off < N_SUB)

        @pl.when(there)
        def _():
            for copy in pair:
                copy.wait_send()

        @pl.when(from_there)
        def _():
            for copy in pair:
                copy.wait_recv()


def send_terms(table, lefts, rights):
    return pl.pallas_call(
        term_kernel,
        out_shape=(pltpu.VMEM((BUCKETS, B, B), I16), pltpu.VMEM((BUCKETS, 1, B), F32)),
        in_specs=[SMEM, VMEM, VMEM],
        out_specs=(VMEM, VMEM),
        scratch_shapes=[
            pltpu.VMEM((CHUNKS, B, B), F32),
            pltpu.VMEM((BUCKETS, B, B), I16),
            pltpu.VMEM((BUCKETS, 1, B), F32),
            pltpu.SemaphoreType.DMA((4, BUCKETS)),
        ],
        compiler_params=pltpu.CompilerParams(collective_id=1, has_side_effects=True, vmem_limit_bytes=22 * MIB),
        name="send_terms",
    )(table, in_vmem(lefts), in_vmem(rights))


def place_kernel(targets_hbm, received, scales, out_hbm, targets, out, sems):
    g = lax.axis_index("group")
    s = lax.axis_index("sub")
    load = pltpu.make_async_copy(targets_hbm, targets, sems.at[0])
    load.start()
    out[...] = jnp.zeros_like(out)
    load.wait()
    for dg in range(N_GROUP):
        sg = group_at(g, dg)
        for off in range(-2, 3):
            j = dg * WIN + off + 2
            ss = s - off
            inside = jnp.logical_and(ss >= 0, ss < N_SUB)
            o = jnp.where(inside, targets[sg * N_SUB + jnp.clip(ss, 0, N_SUB - 1)], OWN)
            block = received[j].astype(jnp.int32).astype(F32) * scales[j]
            out[o] += jnp.where(inside, block, 0.0)
    save = pltpu.make_async_copy(out.at[pl.ds(0, OWN)], out_hbm, sems.at[1])
    save.start()
    save.wait()


def place(targets, received, scales):
    return pl.pallas_call(
        place_kernel,
        out_shape=jax.ShapeDtypeStruct((OWN, B, B), F32),
        in_specs=[HBM, VMEM, VMEM],
        out_specs=HBM,
        scratch_shapes=[
            pltpu.SMEM((N_GROUP * N_SUB,), jnp.int32),
            pltpu.VMEM((OWN + 1, B, B), F32),
            pltpu.SemaphoreType.DMA((2,)),
        ],
        name="place",
    )(in_hbm(targets), in_vmem(received), in_vmem(scales))


def per_device(a_vals, a_cols, p_vals, halo_send, send_slot, recv_block):
    lefts, rights, table = left_blocks(
        a_cols.T, send_slot.transpose(1, 2, 3, 0), halo_send, a_vals, p_vals.reshape(OWN_BLOCKS, B, B)
    )
    received, scales = send_terms(table.reshape(-1), lefts, rights)
    return place(recv_block, received, scales)


def solution(mesh):
    return jax.shard_map(
        per_device,
        mesh=mesh,
        in_specs=(
            P(("group", "sub"), None, None, None),
            P(("group", "sub"), None),
            P(("group", "sub"), None, None, None),
            P(("group", "sub")),
            P(("group", "sub"), None, None, None),
            P(("group", "sub")),
        ),
        out_specs=P(("group", "sub"), None, None),
        check_vma=False,
    )
```

```python
import functools

import jax
import jax.numpy as jnp
from jax import lax
from jax.experimental import pallas as pl
from jax.experimental.pallas import tpu as pltpu
from jax.sharding import PartitionSpec as P

B = 128
ROWS = 32
SLOTS_A = 9
SLOTS_P = 2
HALO = 8
OWN = 32
N_GROUP = 4
N_SUB = 32
ENTRIES = ROWS * SLOTS_A
TERMS = ENTRIES * 4
WIN = 5
BUCKETS = N_GROUP * WIN
ROW_STEP = 4
ROW_RING = 16
U = 4
G = 154
STEPS = 2
STEP_ROWS = 5
KEEP_ROWS = 2
LEFTS = 2 * ENTRIES + 8
OWN_BLOCKS = ROWS * SLOTS_P
FAR_BLOCKS = 2 * HALO * SLOTS_P
RIGHTS = 128
WIDTH = 32
WORD_ROWS = 16
LAST_ROW = WORD_ROWS + STEPS * KEEP_ROWS
FROM_ROW = LAST_ROW + 1
TABLE_ROWS = 24
CODE = 32767.0
MIB = 2**20
LIMIT = 54
MESH = pl.DeviceIdType.MESH
BF = jnp.bfloat16
F32 = jnp.float32
I16 = jnp.int16
SMEM = pl.BlockSpec(memory_space=pltpu.SMEM)
VMEM = pl.BlockSpec(memory_space=pltpu.VMEM)
HBM = pl.BlockSpec(memory_space=pltpu.HBM)


def in_hbm(x):
    return pltpu.with_memory_space_constraint(x, pltpu.HBM)


def in_vmem(x):
    return pltpu.with_memory_space_constraint(x, pltpu.VMEM)


def dot(a, b):
    return jnp.dot(a, b, preferred_element_type=F32)


def group_at(g, d):
    return g + (d % 2) * jnp.where(lax.rem(g, 2) == 0, 1, -1) + (d // 2) * jnp.where(g < 2, 2, -2)


def iota(shape, axis):
    return lax.broadcasted_iota(jnp.int32, shape, axis)


def build_table(g, my_sub, cols, slots, targets, table):
    slot = jnp.concatenate([slots[p, :, q, :] for p in range(SLOTS_P) for q in range(SLOTS_P)], axis=1)
    bucket_of = (slot >> 5) * WIN + ((slot & (N_SUB - 1)) - my_sub + 2)
    known = jnp.logical_and(bucket_of >= 0, bucket_of < BUCKETS)
    col = jnp.concatenate([cols[...]] * 4, axis=1)
    rows = SLOTS_A
    one_hot = [
        (jnp.broadcast_to(bucket_of[r : r + 1, :], (WIDTH, B)) == iota((WIDTH, B), 0)).astype(F32) for r in range(rows)
    ]
    stacked = jnp.concatenate(one_hot, axis=0).astype(BF)
    upper = (iota((B, B), 0) < iota((B, B), 1)).astype(F32).astype(BF)
    rank = dot(stacked, upper)
    total = dot(stacked, jnp.ones((B, B), BF))
    base = jnp.zeros((WIDTH, B), F32)
    ranks = []
    for r in range(rows):
        ranks.append(base + rank[r * WIDTH : (r + 1) * WIDTH])
        base = base + total[r * WIDTH : (r + 1) * WIDTH]
    bucket = iota((WIDTH, B), 0)
    used = ((base.astype(jnp.int32) + (U - 1)) >> (U.bit_length() - 1)).astype(F32)
    used = jnp.where(bucket < BUCKETS, jnp.maximum(used, 1.0), 0.0)
    lower = (iota((WIDTH, WIDTH), 1) < iota((WIDTH, WIDTH), 0)).astype(F32)
    first = jnp.dot(lower, used, precision=lax.Precision.HIGHEST, preferred_element_type=F32)
    lane = iota((1, B), 1)
    i = lane & (ROWS - 1)
    p = lane >> 6
    q = (lane >> 5) & 1
    words = jnp.zeros((3 * WORD_ROWS, B), F32)
    for r in range(rows):
        pos = jnp.sum(one_hot[r] * (first * float(U) + ranks[r]), axis=0, keepdims=True).astype(jnp.int32)
        pos = jnp.where(known[r : r + 1, :], pos, -1)
        step = sum((pos >= n * G * U).astype(jnp.int32) for n in range(1, STEPS))
        pos = pos + step * (STEP_ROWS * B - G * U)
        left = (i * SLOTS_A + r) * 2 + p + 2
        here = jnp.broadcast_to(pos >> 7, (WORD_ROWS, B)) == iota((WORD_ROWS, B), 0)
        parts = [
            jnp.where(here, jnp.broadcast_to(v.astype(F32), (WORD_ROWS, B)), 0.0)
            for v in (col[r : r + 1, :] * 2 + q, left >> 4, left & 15)
        ]
        low = (jnp.broadcast_to(pos & (B - 1), (B, B)) == iota((B, B), 0)).astype(F32).astype(BF)
        words = words + lax.dot_general(
            jnp.concatenate(parts, axis=0).astype(BF),
            low,
            (((1,), (1,)), ((), ())),
            preferred_element_type=F32,
        )
    words = words.astype(jnp.int32)
    table[0:WORD_ROWS, :] = words[:WORD_ROWS] * 1024 + words[WORD_ROWS : 2 * WORD_ROWS] * 16 + words[2 * WORD_ROWS :]
    starts = jnp.where(bucket < BUCKETS, first, -1.0)
    chunk = iota((WIDTH, B), 1).astype(F32)
    keep = [
        1.0 - jnp.sum((starts == chunk + float(n * G + h * B)).astype(F32), axis=0, keepdims=True)
        for n in range(STEPS)
        for h in range(KEEP_ROWS)
    ]
    last = jnp.sum(jnp.where(bucket == iota((WIDTH, B), 1), first + used - 1.0, 0.0), axis=0, keepdims=True)
    away = (lane & (N_SUB - 1)) - my_sub
    near = jnp.logical_and(away >= -2, away <= 2)
    slot = ((lane >> 5) ^ g) * WIN + 2 - away
    owned = jnp.where(near, targets[...], OWN)
    takes = (jnp.broadcast_to(owned, (WIDTH, B)) == bucket).astype(F32)
    order = dot(takes.astype(BF), upper)
    count = dot(takes.astype(BF), jnp.ones((B, B), BF))
    start = dot(lower.astype(BF), count.astype(BF))
    pos = jnp.sum(takes * (start + order), axis=0, keepdims=True).astype(jnp.int32)
    pos = jnp.where(jnp.logical_and(near, owned < OWN), pos, -1)
    spread = (jnp.broadcast_to(pos, (B, B)) == iota((B, B), 0)).astype(F32).astype(BF)
    source = lax.dot_general(
        jnp.broadcast_to(slot.astype(F32), (8, B)).astype(BF),
        spread,
        (((1,), (1,)), ((), ())),
        preferred_element_type=F32,
    )[0:1]
    opens = jnp.where(count > 0.0, start, -1.0)
    join = 1.0 - jnp.sum((opens == chunk).astype(F32), axis=0, keepdims=True)
    final = jnp.where(count > 0.0, start + count - 1.0, float(BUCKETS))
    final = jnp.sum(jnp.where(bucket == iota((WIDTH, B), 1), final, 0.0), axis=0, keepdims=True)
    rest = jnp.concatenate(keep + [last, source, join, final], axis=0)
    table[WORD_ROWS:TABLE_ROWS, :] = rest.astype(jnp.int32)


def terms_kernel(
    cols_hbm, slots_hbm, send_hbm, targets_hbm, a_hbm, p_hbm, out,
    cols, slots, halo_send, targets, a_v, p_v, packed, lefts, rights, table_v, table, run, coded, scale, received, scales,
    a_sems, in_sems, send_sems, recv_sems, sems,
):
    g = lax.axis_index("group")
    s = lax.axis_index("sub")
    sides = ((s > 0, (g, jnp.maximum(s - 1, 0))), (s < N_SUB - 1, (g, jnp.minimum(s + 1, N_SUB - 1))))
    peers = []
    for off in (2, -2, 1, -1, 0):
        for dg in (3, 2, 1, 0):
            if dg or off:
                there = jnp.logical_and(s + off >= 0, s + off < N_SUB)
                ts = jnp.clip(s + off, 0, N_SUB - 1)
                peers.append((dg, off, there, group_at(g, dg), ts))
    load = pltpu.make_async_copy(p_hbm, p_v, in_sems.at[0])
    small = [
        pltpu.make_async_copy(src, dst, in_sems.at[1 + n])
        for n, (src, dst) in enumerate(((send_hbm, halo_send), (cols_hbm, cols), (slots_hbm, slots), (targets_hbm, targets)))
    ]
    small[0].start()
    load.start()
    small[1].start()
    small[2].start()
    small[3].start()
    barrier = pltpu.get_barrier_semaphore()
    for _, _, there, tg, ts in peers:

        @pl.when(there)
        def _():
            pl.semaphore_signal(barrier, inc=1, device_id=(tg, ts), device_id_type=MESH)

    def fetch(i):
        place = lax.rem(i, ROW_RING)
        return pltpu.make_async_copy(a_hbm.at[i], a_v.at[place], a_sems.at[place])

    for i in range(ROW_RING):
        fetch(i).start()
    for copy in small:
        copy.wait()
    zero = jnp.zeros((B, B), BF)
    load.wait()
    for j in range(2 * HALO):
        row = halo_send[j]
        for q in range(SLOTS_P):
            packed[j * 2 + q] = p_v[(row & (ROWS - 1)) * 2 + q]
    half = FAR_BLOCKS // 2
    copies = []
    for n, (there, peer) in enumerate(sides):
        copies.append(
            pltpu.make_async_remote_copy(
                src_ref=packed.at[pl.ds(n * half, half)],
                dst_ref=rights.at[pl.ds(OWN_BLOCKS + half - n * half, half)],
                send_sem=send_sems.at[n],
                recv_sem=recv_sems.at[n],
                device_id=peer,
                device_id_type=MESH,
            )
        )
    pl.semaphore_wait(barrier, sum(peer[2].astype(jnp.int32) for peer in peers))
    for (there, _), copy in zip(sides, copies):

        @pl.when(there)
        def _():
            copy.start()

    lefts[0] = zero
    lefts[1] = zero
    build_table(g, s, cols, slots, targets, table_v)
    move = pltpu.make_async_copy(table_v, table, in_sems.at[5])
    move.start()

    @pl.loop(0, ROWS // ROW_STEP)
    def _(step):
        for r in range(ROW_STEP):
            fetch(step * ROW_STEP + r).wait()
        for r in range(ROW_STEP):
            i = step * ROW_STEP + r
            place = lax.rem(i, ROW_RING)
            p_t = jnp.concatenate([p_v[i * 2].T, p_v[i * 2 + 1].T], axis=0)
            for p in range(SLOTS_P):
                rights[i * 2 + p] = p_v[i * 2 + p]
            first = i * (2 * SLOTS_A) + 2
            for k in range(0, SLOTS_A - 1, 2):
                y = dot(p_t, jnp.concatenate([a_v[place, k], a_v[place, k + 1]], axis=1)).astype(BF)
                for n in range(2):
                    for p in range(SLOTS_P):
                        lefts[first + (k + n) * 2 + p] = y[p * B : (p + 1) * B, n * B : (n + 1) * B]
            k = SLOTS_A - 1
            both = jnp.concatenate([p_t[:B], p_t[B:]], axis=1)
            top = jnp.concatenate([a_v[place, k], zero], axis=1)
            bottom = jnp.concatenate([zero, a_v[place, k]], axis=1)
            y = dot(both, jnp.concatenate([top, bottom], axis=0)).astype(BF)
            for p in range(SLOTS_P):
                lefts[first + k * 2 + p] = y[:, p * B : (p + 1) * B]
        for r in range(ROW_STEP):
            i = step * ROW_STEP + r + ROW_RING

            @pl.when(i < ROWS)
            def _():
                fetch(i).start()

    move.wait()
    for n, (there, _) in enumerate(sides):

        @pl.when(there)
        def _():
            copies[n].wait_send()
            copies[1 - n].wait_recv()

        @pl.when(jnp.logical_not(there))
        def _():
            rights[pl.ds(OWN_BLOCKS + n * half, half)] = jnp.zeros((half, B, B), BF)

    def step(it, acc):
        for n in range(G):
            left, right = [], []
            for u in range(n * U, n * U + U):
                w = table[it * STEP_ROWS + u // B, u % B]
                left.append(lefts[jnp.minimum(w & 1023, LEFTS - 1)])
                right.append(rights[(w >> 10) & (RIGHTS - 1)])
            keep = table[WORD_ROWS + it * KEEP_ROWS + n // B, n % B].astype(F32)
            acc = acc * keep + dot(jnp.concatenate(left, axis=1), jnp.concatenate(right, axis=0))
            run[it * G + n] = acc
        return acc

    lax.fori_loop(0, STEPS, step, jnp.zeros((B, B), F32))

    def code(bucket):
        total = run[jnp.clip(table[LAST_ROW, bucket], 0, STEPS * G - 1)]
        top = jnp.maximum(jnp.max(jnp.abs(total), axis=0, keepdims=True), 1e-30)
        return jnp.round(total * (CODE / top)).astype(jnp.int32).astype(I16), top * (1.0 / CODE)


    copies = []
    for dg, off, there, tg, ts in peers:
        j = dg * WIN + off + 2
        pair = [
            pltpu.make_async_remote_copy(
                src_ref=src.at[j],
                dst_ref=dst.at[j],
                send_sem=sems.at[2 * n, j],
                recv_sem=sems.at[2 * n + 1, j],
                device_id=(tg, ts),
                device_id_type=MESH,
            )
            for n, (src, dst) in enumerate(((coded, received), (scale, scales)))
        ]
        copies.append(pair)

        @pl.when(there)
        def _():
            coded[j], scale[j] = code(tg * WIN + (off + 2))
            for copy in pair:
                copy.start()

    received[2], scales[2] = code(g * WIN + 2)
    for (dg, off, there, _, _), pair in zip(peers, copies):
        from_there = jnp.logical_and(s - off >= 0, s - off < N_SUB)

        @pl.when(there)
        def _():
            for copy in pair:
                copy.wait_send()

        @pl.when(from_there)
        def _():
            for copy in pair:
                copy.wait_recv()

    acc = jnp.zeros((B, B), F32)
    run[BUCKETS] = acc
    for n in range(BUCKETS):
        j = jnp.clip(table[FROM_ROW, n], 0, BUCKETS - 1)
        acc = acc * table[FROM_ROW + 1, n].astype(F32) + received[j].astype(jnp.int32).astype(F32) * scales[j]
        run[n] = acc
    for o in range(OWN):
        out[o] = run[jnp.clip(table[FROM_ROW + 2, o], 0, BUCKETS)]


def sum_terms(cols, slots, halo_send, targets, a_vals, p_blocks):
    return pl.pallas_call(
        terms_kernel,
        out_shape=pltpu.VMEM((OWN, B, B), F32),
        in_specs=[HBM] * 6,
        out_specs=VMEM,
        scratch_shapes=[
            pltpu.VMEM((SLOTS_A, ROWS), jnp.int32),
            pltpu.VMEM((SLOTS_P, SLOTS_A, SLOTS_P, ROWS), jnp.int32),
            pltpu.SMEM((2 * HALO,), jnp.int32),
            pltpu.VMEM((1, N_GROUP * N_SUB), jnp.int32),
            pltpu.VMEM((ROW_RING, SLOTS_A, B, B), BF),
            pltpu.VMEM((OWN_BLOCKS, B, B), BF),
            pltpu.VMEM((FAR_BLOCKS, B, B), BF),
            pltpu.VMEM((LEFTS, B, B), BF),
            pltpu.VMEM((RIGHTS, B, B), BF),
            pltpu.VMEM((TABLE_ROWS, B), jnp.int32),
            pltpu.SMEM((TABLE_ROWS, B), jnp.int32),
            pltpu.VMEM((STEPS * G, B, B), F32),
            pltpu.VMEM((BUCKETS, B, B), I16),
            pltpu.VMEM((BUCKETS, 1, B), F32),
            pltpu.VMEM((BUCKETS, B, B), I16),
            pltpu.VMEM((BUCKETS, 1, B), F32),
            pltpu.SemaphoreType.DMA((ROW_RING,)),
            pltpu.SemaphoreType.DMA((6,)),
            pltpu.SemaphoreType.DMA((2,)),
            pltpu.SemaphoreType.DMA((2,)),
            pltpu.SemaphoreType.DMA((4, BUCKETS)),
        ],
        compiler_params=pltpu.CompilerParams(collective_id=0, has_side_effects=True, vmem_limit_bytes=LIMIT * MIB),
        name="sum_terms",
    )(*[in_hbm(x) for x in (cols, slots, halo_send, targets, a_vals, p_blocks)])


def per_device(a_vals, a_cols, p_vals, halo_send, send_slot, recv_block):
    slots = send_slot.transpose(1, 2, 3, 0)
    targets = recv_block.reshape(1, -1)
    return sum_terms(a_cols.T, slots, halo_send, targets, a_vals, p_vals.reshape(OWN_BLOCKS, B, B))


def solution(mesh):
    return jax.shard_map(
        per_device,
        mesh=mesh,
        in_specs=(
            P(("group", "sub"), None, None, None),
            P(("group", "sub"), None),
            P(("group", "sub"), None, None, None),
            P(("group", "sub")),
            P(("group", "sub"), None, None, None),
            P(("group", "sub")),
        ),
        out_specs=P(("group", "sub"), None, None),
        check_vma=False,
    )
```

```python
import functools

import jax
import jax.numpy as jnp
from jax import lax
from jax.experimental import pallas as pl
from jax.experimental.pallas import tpu as pltpu
from jax.sharding import PartitionSpec as P

B = 128
ROWS = 32
SLOTS_A = 9
SLOTS_P = 2
HALO = 8
OWN = 32
N_GROUP = 4
N_SUB = 32
ENTRIES = ROWS * SLOTS_A
TERMS = ENTRIES * 4
WIN = 5
BUCKETS = N_GROUP * WIN
ROW_STEP = 4
ROW_RING = 16
U = 4
G = 308
STEPS = 1
STEP_ROWS = 10
KEEP_ROWS = 4
LEFTS = 2 * ENTRIES + 8
OWN_BLOCKS = ROWS * SLOTS_P
FAR_BLOCKS = 2 * HALO * SLOTS_P
RIGHTS = 128
WIDTH = 32
WORD_ROWS = 16
LAST_ROW = WORD_ROWS + STEPS * KEEP_ROWS
FROM_ROW = LAST_ROW + 1
TABLE_ROWS = 24
CODE = 32767.0
MIB = 2**20
LIMIT = 54
MESH = pl.DeviceIdType.MESH
BF = jnp.bfloat16
F32 = jnp.float32
I16 = jnp.int16
SMEM = pl.BlockSpec(memory_space=pltpu.SMEM)
VMEM = pl.BlockSpec(memory_space=pltpu.VMEM)
HBM = pl.BlockSpec(memory_space=pltpu.HBM)


def in_hbm(x):
    return pltpu.with_memory_space_constraint(x, pltpu.HBM)


def in_vmem(x):
    return pltpu.with_memory_space_constraint(x, pltpu.VMEM)


def dot(a, b):
    return jnp.dot(a, b, preferred_element_type=F32)


def group_at(g, d):
    return g + (d % 2) * jnp.where(lax.rem(g, 2) == 0, 1, -1) + (d // 2) * jnp.where(g < 2, 2, -2)


def iota(shape, axis):
    return lax.broadcasted_iota(jnp.int32, shape, axis)


def build_table(g, my_sub, cols, slots, targets, table):
    slot = jnp.concatenate([slots[p, :, q, :] for p in range(SLOTS_P) for q in range(SLOTS_P)], axis=1)
    bucket_of = (slot >> 5) * WIN + ((slot & (N_SUB - 1)) - my_sub + 2)
    known = jnp.logical_and(bucket_of >= 0, bucket_of < BUCKETS)
    col = jnp.concatenate([cols[...]] * 4, axis=1)
    rows = SLOTS_A
    one_hot = [
        (jnp.broadcast_to(bucket_of[r : r + 1, :], (WIDTH, B)) == iota((WIDTH, B), 0)).astype(F32) for r in range(rows)
    ]
    stacked = jnp.concatenate(one_hot, axis=0).astype(BF)
    upper = (iota((B, B), 0) < iota((B, B), 1)).astype(F32).astype(BF)
    rank = dot(stacked, upper)
    total = dot(stacked, jnp.ones((B, B), BF))
    base = jnp.zeros((WIDTH, B), F32)
    ranks = []
    for r in range(rows):
        ranks.append(base + rank[r * WIDTH : (r + 1) * WIDTH])
        base = base + total[r * WIDTH : (r + 1) * WIDTH]
    bucket = iota((WIDTH, B), 0)
    used = ((base.astype(jnp.int32) + (U - 1)) >> (U.bit_length() - 1)).astype(F32)
    used = jnp.where(bucket < BUCKETS, jnp.maximum(used, 1.0), 0.0)
    lower = (iota((WIDTH, WIDTH), 1) < iota((WIDTH, WIDTH), 0)).astype(F32)
    first = jnp.dot(lower, used, precision=lax.Precision.HIGHEST, preferred_element_type=F32)
    lane = iota((1, B), 1)
    i = lane & (ROWS - 1)
    p = lane >> 6
    q = (lane >> 5) & 1
    words = jnp.zeros((3 * WORD_ROWS, B), F32)
    for r in range(rows):
        pos = jnp.sum(one_hot[r] * (first * float(U) + ranks[r]), axis=0, keepdims=True).astype(jnp.int32)
        pos = jnp.where(known[r : r + 1, :], pos, -1)
        step = sum((pos >= n * G * U).astype(jnp.int32) for n in range(1, STEPS))
        pos = pos + step * (STEP_ROWS * B - G * U)
        left = (i * SLOTS_A + r) * 2 + p + 2
        here = jnp.broadcast_to(pos >> 7, (WORD_ROWS, B)) == iota((WORD_ROWS, B), 0)
        parts = [
            jnp.where(here, jnp.broadcast_to(v.astype(F32), (WORD_ROWS, B)), 0.0)
            for v in (col[r : r + 1, :] * 2 + q, left >> 4, left & 15)
        ]
        low = (jnp.broadcast_to(pos & (B - 1), (B, B)) == iota((B, B), 0)).astype(F32).astype(BF)
        words = words + lax.dot_general(
            jnp.concatenate(parts, axis=0).astype(BF),
            low,
            (((1,), (1,)), ((), ())),
            preferred_element_type=F32,
        )
    words = words.astype(jnp.int32)
    table[0:WORD_ROWS, :] = words[:WORD_ROWS] * 1024 + words[WORD_ROWS : 2 * WORD_ROWS] * 16 + words[2 * WORD_ROWS :]
    starts = jnp.where(bucket < BUCKETS, first, -1.0)
    chunk = iota((WIDTH, B), 1).astype(F32)
    keep = [
        1.0 - jnp.sum((starts == chunk + float(n * G + h * B)).astype(F32), axis=0, keepdims=True)
        for n in range(STEPS)
        for h in range(KEEP_ROWS)
    ]
    last = jnp.sum(jnp.where(bucket == iota((WIDTH, B), 1), first + used - 1.0, 0.0), axis=0, keepdims=True)
    away = (lane & (N_SUB - 1)) - my_sub
    near = jnp.logical_and(away >= -2, away <= 2)
    slot = ((lane >> 5) ^ g) * WIN + 2 - away
    owned = jnp.where(near, targets[...], OWN)
    takes = (jnp.broadcast_to(owned, (WIDTH, B)) == bucket).astype(F32)
    order = dot(takes.astype(BF), upper)
    count = dot(takes.astype(BF), jnp.ones((B, B), BF))
    start = dot(lower.astype(BF), count.astype(BF))
    pos = jnp.sum(takes * (start + order), axis=0, keepdims=True).astype(jnp.int32)
    pos = jnp.where(jnp.logical_and(near, owned < OWN), pos, -1)
    spread = (jnp.broadcast_to(pos, (B, B)) == iota((B, B), 0)).astype(F32).astype(BF)
    source = lax.dot_general(
        jnp.broadcast_to(slot.astype(F32), (8, B)).astype(BF),
        spread,
        (((1,), (1,)), ((), ())),
        preferred_element_type=F32,
    )[0:1]
    opens = jnp.where(count > 0.0, start, -1.0)
    join = 1.0 - jnp.sum((opens == chunk).astype(F32), axis=0, keepdims=True)
    final = jnp.where(count > 0.0, start + count - 1.0, float(BUCKETS))
    final = jnp.sum(jnp.where(bucket == iota((WIDTH, B), 1), final, 0.0), axis=0, keepdims=True)
    rest = jnp.concatenate(keep + [last, source, join, final], axis=0)
    table[WORD_ROWS:TABLE_ROWS, :] = rest.astype(jnp.int32)


def terms_kernel(
    cols_hbm, slots_hbm, send_hbm, targets_hbm, a_hbm, p_hbm, out,
    cols, slots, halo_send, targets, a_v, p_v, packed, lefts, rights, table_v, table, run, coded, scale, received, scales,
    a_sems, in_sems, send_sems, recv_sems, sems,
):
    g = lax.axis_index("group")
    s = lax.axis_index("sub")
    sides = ((s > 0, (g, jnp.maximum(s - 1, 0))), (s < N_SUB - 1, (g, jnp.minimum(s + 1, N_SUB - 1))))
    peers = []
    for off in (2, -2, 1, -1, 0):
        for dg in (3, 2, 1, 0):
            if dg or off:
                there = jnp.logical_and(s + off >= 0, s + off < N_SUB)
                ts = jnp.clip(s + off, 0, N_SUB - 1)
                peers.append((dg, off, there, group_at(g, dg), ts))
    load = pltpu.make_async_copy(p_hbm, p_v, in_sems.at[0])
    small = [
        pltpu.make_async_copy(src, dst, in_sems.at[1 + n])
        for n, (src, dst) in enumerate(((send_hbm, halo_send), (cols_hbm, cols), (slots_hbm, slots), (targets_hbm, targets)))
    ]
    small[0].start()
    load.start()
    small[1].start()
    small[2].start()
    small[3].start()
    barrier = pltpu.get_barrier_semaphore()
    for _, _, there, tg, ts in peers:

        @pl.when(there)
        def _():
            pl.semaphore_signal(barrier, inc=1, device_id=(tg, ts), device_id_type=MESH)

    def fetch(i):
        place = lax.rem(i, ROW_RING)
        return pltpu.make_async_copy(a_hbm.at[i], a_v.at[place], a_sems.at[place])

    for i in range(ROW_RING):
        fetch(i).start()
    for copy in small:
        copy.wait()
    zero = jnp.zeros((B, B), BF)
    load.wait()
    for j in range(2 * HALO):
        row = halo_send[j]
        for q in range(SLOTS_P):
            packed[j * 2 + q] = p_v[(row & (ROWS - 1)) * 2 + q]
    half = FAR_BLOCKS // 2
    copies = []
    for n, (there, peer) in enumerate(sides):
        copies.append(
            pltpu.make_async_remote_copy(
                src_ref=packed.at[pl.ds(n * half, half)],
                dst_ref=rights.at[pl.ds(OWN_BLOCKS + half - n * half, half)],
                send_sem=send_sems.at[n],
                recv_sem=recv_sems.at[n],
                device_id=peer,
                device_id_type=MESH,
            )
        )
    pl.semaphore_wait(barrier, sum(peer[2].astype(jnp.int32) for peer in peers))
    for (there, _), copy in zip(sides, copies):

        @pl.when(there)
        def _():
            copy.start()

    lefts[0] = zero
    lefts[1] = zero
    build_table(g, s, cols, slots, targets, table_v)
    move = pltpu.make_async_copy(table_v, table, in_sems.at[5])
    move.start()

    @pl.loop(0, ROWS // ROW_STEP)
    def _(step):
        for r in range(ROW_STEP):
            fetch(step * ROW_STEP + r).wait()
        for r in range(ROW_STEP):
            i = step * ROW_STEP + r
            place = lax.rem(i, ROW_RING)
            p_t = jnp.concatenate([p_v[i * 2].T, p_v[i * 2 + 1].T], axis=0)
            for p in range(SLOTS_P):
                rights[i * 2 + p] = p_v[i * 2 + p]
            first = i * (2 * SLOTS_A) + 2
            for k in range(0, SLOTS_A - 1, 2):
                y = dot(p_t, jnp.concatenate([a_v[place, k], a_v[place, k + 1]], axis=1)).astype(BF)
                for n in range(2):
                    for p in range(SLOTS_P):
                        lefts[first + (k + n) * 2 + p] = y[p * B : (p + 1) * B, n * B : (n + 1) * B]
            k = SLOTS_A - 1
            both = jnp.concatenate([p_t[:B], p_t[B:]], axis=1)
            top = jnp.concatenate([a_v[place, k], zero], axis=1)
            bottom = jnp.concatenate([zero, a_v[place, k]], axis=1)
            y = dot(both, jnp.concatenate([top, bottom], axis=0)).astype(BF)
            for p in range(SLOTS_P):
                lefts[first + k * 2 + p] = y[:, p * B : (p + 1) * B]
        for r in range(ROW_STEP):
            i = step * ROW_STEP + r + ROW_RING

            @pl.when(i < ROWS)
            def _():
                fetch(i).start()

    move.wait()
    for n, (there, _) in enumerate(sides):

        @pl.when(there)
        def _():
            copies[n].wait_send()
            copies[1 - n].wait_recv()

        @pl.when(jnp.logical_not(there))
        def _():
            rights[pl.ds(OWN_BLOCKS + n * half, half)] = jnp.zeros((half, B, B), BF)

    def step(it, acc):
        for n in range(G):
            left, right = [], []
            for u in range(n * U, n * U + U):
                w = table[it * STEP_ROWS + u // B, u % B]
                left.append(lefts[jnp.minimum(w & 1023, LEFTS - 1)])
                right.append(rights[(w >> 10) & (RIGHTS - 1)])
            keep = table[WORD_ROWS + it * KEEP_ROWS + n // B, n % B].astype(F32)
            acc = acc * keep + dot(jnp.concatenate(left, axis=1), jnp.concatenate(right, axis=0))
            run[it * G + n] = acc
        return acc

    lax.fori_loop(0, STEPS, step, jnp.zeros((B, B), F32))

    def code(bucket):
        total = run[jnp.clip(table[LAST_ROW, bucket], 0, STEPS * G - 1)]
        top = jnp.maximum(jnp.max(jnp.abs(total), axis=0, keepdims=True), 1e-30)
        return jnp.round(total * (CODE / top)).astype(jnp.int32).astype(I16), top * (1.0 / CODE)


    copies = []
    for dg, off, there, tg, ts in peers:
        j = dg * WIN + off + 2
        pair = [
            pltpu.make_async_remote_copy(
                src_ref=src.at[j],
                dst_ref=dst.at[j],
                send_sem=sems.at[2 * n, j],
                recv_sem=sems.at[2 * n + 1, j],
                device_id=(tg, ts),
                device_id_type=MESH,
            )
            for n, (src, dst) in enumerate(((coded, received), (scale, scales)))
        ]
        copies.append(pair)

        @pl.when(there)
        def _():
            coded[j], scale[j] = code(tg * WIN + (off + 2))
            for copy in pair:
                copy.start()

    received[2], scales[2] = code(g * WIN + 2)
    for (dg, off, there, _, _), pair in zip(peers, copies):
        from_there = jnp.logical_and(s - off >= 0, s - off < N_SUB)

        @pl.when(there)
        def _():
            for copy in pair:
                copy.wait_send()

        @pl.when(from_there)
        def _():
            for copy in pair:
                copy.wait_recv()

    acc = jnp.zeros((B, B), F32)
    run[BUCKETS] = acc
    for n in range(BUCKETS):
        j = jnp.clip(table[FROM_ROW, n], 0, BUCKETS - 1)
        acc = acc * table[FROM_ROW + 1, n].astype(F32) + received[j].astype(jnp.int32).astype(F32) * scales[j]
        run[n] = acc
    for o in range(OWN):
        out[o] = run[jnp.clip(table[FROM_ROW + 2, o], 0, BUCKETS)]


def sum_terms(cols, slots, halo_send, targets, a_vals, p_blocks):
    return pl.pallas_call(
        terms_kernel,
        out_shape=pltpu.VMEM((OWN, B, B), F32),
        in_specs=[HBM] * 6,
        out_specs=VMEM,
        scratch_shapes=[
            pltpu.VMEM((SLOTS_A, ROWS), jnp.int32),
            pltpu.VMEM((SLOTS_P, SLOTS_A, SLOTS_P, ROWS), jnp.int32),
            pltpu.SMEM((2 * HALO,), jnp.int32),
            pltpu.VMEM((1, N_GROUP * N_SUB), jnp.int32),
            pltpu.VMEM((ROW_RING, SLOTS_A, B, B), BF),
            pltpu.VMEM((OWN_BLOCKS, B, B), BF),
            pltpu.VMEM((FAR_BLOCKS, B, B), BF),
            pltpu.VMEM((LEFTS, B, B), BF),
            pltpu.VMEM((RIGHTS, B, B), BF),
            pltpu.VMEM((TABLE_ROWS, B), jnp.int32),
            pltpu.SMEM((TABLE_ROWS, B), jnp.int32),
            pltpu.VMEM((STEPS * G, B, B), F32),
            pltpu.VMEM((BUCKETS, B, B), I16),
            pltpu.VMEM((BUCKETS, 1, B), F32),
            pltpu.VMEM((BUCKETS, B, B), I16),
            pltpu.VMEM((BUCKETS, 1, B), F32),
            pltpu.SemaphoreType.DMA((ROW_RING,)),
            pltpu.SemaphoreType.DMA((6,)),
            pltpu.SemaphoreType.DMA((2,)),
            pltpu.SemaphoreType.DMA((2,)),
            pltpu.SemaphoreType.DMA((4, BUCKETS)),
        ],
        compiler_params=pltpu.CompilerParams(collective_id=0, has_side_effects=True, vmem_limit_bytes=LIMIT * MIB),
        name="sum_terms",
    )(*[in_hbm(x) for x in (cols, slots, halo_send, targets, a_vals, p_blocks)])


def per_device(a_vals, a_cols, p_vals, halo_send, send_slot, recv_block):
    slots = send_slot.transpose(1, 2, 3, 0)
    targets = recv_block.reshape(1, -1)
    return sum_terms(a_cols.T, slots, halo_send, targets, a_vals, p_vals.reshape(OWN_BLOCKS, B, B))


def solution(mesh):
    return jax.shard_map(
        per_device,
        mesh=mesh,
        in_specs=(
            P(("group", "sub"), None, None, None),
            P(("group", "sub"), None),
            P(("group", "sub"), None, None, None),
            P(("group", "sub")),
            P(("group", "sub"), None, None, None),
            P(("group", "sub")),
        ),
        out_specs=P(("group", "sub"), None, None),
        check_vma=False,
    )
```
